32 devices in a mesh: groups: 2 (over y), pair: 4 (over z), mm: 2 (over x), sub: 2 (over core).
Axes of the slice: x: 2, y: 2, z: 4, core: 2. Of those that a mesh axis runs over, the one named last changes fastest.
Arguments:
- centers: float32 [256, 3, 128], P(('groups', 'pair', 'sub')), parts along dimension 0, may hold values from -6 to 6
- widths: float32 [256, 128], P(('groups', 'pair', 'sub')), parts along dimension 0, may hold values from 0.2 to 2
- density: float32 [256, 128], P(('groups', 'pair', 'sub')), parts along dimension 0, may hold values from -0.3 to 0.3
- prefactor: float32 [256, 128], P(('groups', 'pair', 'sub')), parts along dimension 0, may hold values from 0.2 to 2
- padding: int32 [256], P(('groups', 'pair', 'sub')), parts along dimension 0, may hold values from 0 to 64
- pattern: int32 [256, 2, 16], P(('groups', 'pair', 'sub'), 'mm'), parts along dimension 0, may hold values from 0 to 255, as said below
- mm_coords: float32 [512, 2, 3, 128], P(('groups', 'pair'), 'mm'), parts along dimension 0, may hold values from -6 to 6
- mm_charges: float32 [512, 2, 128], P(('groups', 'pair'), 'mm'), parts along dimension 0, may hold values from -1 to 1
Outputs:
- mm_force: float32 [512, 2, 3, 128], P(('groups', 'pair'), 'mm'), parts along dimension 0
- tile_force: float32 [256, 3, 128], P(('groups', 'pair', 'sub')), parts along dimension 0
The draws below stay inside these ranges and needn't reach their ends.
There are 2 independent parts, one for each index of `groups`. The reference program is written for one: setup_inputs(seed, part) draws one part's arguments, and reference() takes and returns one part's arrays. A program takes and returns all parts, laid end to end along the dimension named above; each array names one. Nothing has to cross between parts.
Inputs may be any that keep to these rules, and one draw needn't show every extreme that they name: `pattern`: values index the 256 blocks of the slot's MM group and may repeat within a tile. Block b belongs to pair index b // 64. Among the 256 slots of one device's tiles (an aligned run of 16 tiles) for one MM group, at most 128 name blocks of one pair index, and in each such run some pair index is named exactly 128 times.
All inputs are finite; a program needn't handle non-finite values.
Results may differ from the reference program's by a relative error of at most 0.00016.
Values sent between devices are 32-bit elements; how exact they have to be, the bound alone decides.
A program may use at most 64 MiB of HBM per device.

```python
import math
import jax
import jax.numpy as jnp
from jax import lax

PAIRS = 128
ATOMS = 128
NEAR = 16
TILES_DEV = 16
BLK_DEV = 64
TILES = 128
BLK_GRP = 256
CAP = 128
N_MM = 2


def draw_pattern(key, part):
    key = jax.random.fold_in(key, 7)
    owners = BLK_GRP // BLK_DEV
    shards = TILES // TILES_DEV
    rows = TILES_DEV * NEAR
    count = shards * N_MM
    key_hot, key_off, key_perm, key_local = jax.random.split(key, 4)
    hot = jax.random.randint(key_hot, (count, 1), 0, owners)
    offset = jax.random.randint(key_off, (count, 1), 0, owners - 1)
    position = jnp.arange(rows, dtype=jnp.int32)[None, :]
    spread = (hot + 1 + (offset + position - CAP) % (owners - 1)) % owners
    dest = jnp.where(position < CAP, hot, spread)
    order = jax.vmap(lambda k: jax.random.permutation(k, rows))(jax.random.split(key_perm, count))
    dest = jnp.take_along_axis(dest, order.astype(jnp.int32), axis=1)
    local = jax.random.randint(key_local, (count, rows), 0, BLK_DEV)
    value = dest * BLK_DEV + local
    value = value.reshape(shards, N_MM, TILES_DEV, NEAR).transpose(0, 2, 1, 3)
    return value.reshape(TILES, N_MM, NEAR).astype(jnp.int32)


def with_ends(entries, key, low, high):
    spot = [jax.random.randint(jax.random.fold_in(key, axis), (), 0, length) for axis, length in enumerate(entries.shape)]
    widest = entries.shape.index(max(entries.shape))
    next_to = spot[:widest] + [(spot[widest] + 1) % entries.shape[widest]] + spot[widest + 1:]
    return entries.at[tuple(spot)].set(low).at[tuple(next_to)].set(high)


def steps_of(rng, extent, cuts, low, largest):
    level = 1.0
    for dim, blocks in cuts:
        heights = jax.random.uniform(jax.random.fold_in(jax.random.fold_in(rng, 6), dim), (blocks,), jnp.float32, low / len(cuts), largest / len(cuts))
        level = level * jnp.repeat(jnp.exp(heights), extent[dim] // blocks).reshape((-1,) + (1,) * (len(extent) - 1 - dim))
    return level


def scatter_about(key, shape, scale, bound, cuts=(), held_as=jnp.bfloat16):
    entries = jax.random.normal(key, shape, jnp.float32) * scale
    if len(cuts) > 0:
        entries = steps_of(key, shape, cuts, -0.22, 0.18) * entries
    return jnp.clip(entries, min=-bound, max=bound).astype(held_as)


def setup_inputs(seed: int = 0, part: int = 0) -> dict:
    seeds = jax.random.split(jax.random.key(seed), 9)
    own_keys = jax.random.split(jax.random.fold_in(seeds[8], part), 9)
    centers = scatter_about(own_keys[0], (TILES, 3, PAIRS), 1.0, 6.0, ((0, 8),), jnp.float32)
    widths = jnp.clip(jnp.exp(math.log(2.0) - 2.3025851 * jax.random.uniform(own_keys[1], (TILES, PAIRS), jnp.float32) ** steps_of(own_keys[1], (TILES, PAIRS), ((0, 8),), -0.2, 0.2)), 0.2, 2.0)
    density = scatter_about(own_keys[2], (TILES, PAIRS), 0.05, 0.3, ((0, 8),), jnp.float32)
    prefactor = jnp.clip(jnp.exp(math.log(2.0) - 2.3025851 * jax.random.uniform(own_keys[3], (TILES, PAIRS), jnp.float32) ** steps_of(own_keys[3], (TILES, PAIRS), ((0, 8),), -0.2, 0.2)), 0.2, 2.0)
    padding = with_ends(jax.random.randint(own_keys[4], (TILES,), 0, PAIRS // 2 + 1), jax.random.fold_in(own_keys[4], 1), 0, (PAIRS // 2 + 1) - 1).astype(jnp.int32)
    pattern = draw_pattern(jax.random.fold_in(jax.random.fold_in(seeds[8], part), 71), part)
    mm_coords = scatter_about(own_keys[6], (BLK_GRP, N_MM, 3, ATOMS), 1.0, 6.0, ((0, 4), (1, 2)), jnp.float32)
    mm_charges = jnp.clip(jax.random.uniform(own_keys[7], (BLK_GRP, N_MM, ATOMS), jnp.float32, -1.0, 1.0) * steps_of(own_keys[7], (BLK_GRP, N_MM, ATOMS), ((0, 4), (1, 2)), -0.4, 0.0), -1.0, 1.0)
    return {"centers": centers, "widths": widths, "density": density, "prefactor": prefactor, "padding": padding, "pattern": pattern, "mm_coords": mm_coords, "mm_charges": mm_charges}


def interact(centers, widths, weight, coords, charges):
    delta_sq = jnp.sum((coords[:, None, :] - centers[:, :, None]) ** 2, axis=0)
    coef = weight[:, None] * charges[None, :] * (delta_sq + widths[:, None]) ** -1.5
    col_total = jnp.sum(coef, axis=0)
    row_total = jnp.sum(coef, axis=1)
    cross_atoms = jnp.dot(centers, coef, precision=lax.Precision.HIGHEST)
    cross_pairs = jnp.dot(coords, coef.T, precision=lax.Precision.HIGHEST)
    mm_term = coords * col_total[None, :] - cross_atoms
    center_term = centers * row_total[None, :] - cross_pairs
    return mm_term, center_term


def reference(centers, widths, density, prefactor, padding, pattern, mm_coords, mm_charges):
    slots = jnp.arange(PAIRS, dtype=jnp.int32)[None, :]
    weight = jnp.where(slots < (PAIRS - padding)[:, None], density * prefactor, jnp.float32(0.0))
    group_ids = jnp.broadcast_to(jnp.arange(N_MM, dtype=jnp.int32)[:, None], (N_MM, NEAR))
    inner = jax.vmap(jax.vmap(interact, (None, None, None, 0, 0)), (None, None, None, 0, 0))

    def per_tile(carry, items):
        cen, wid, wgt, pat = items
        crd = mm_coords[pat, group_ids]
        chg = mm_charges[pat, group_ids]
        mm_term, center_term = inner(cen, wid, wgt, crd, chg)
        carry = carry.at[pat, group_ids].add(mm_term)
        return carry, jnp.sum(center_term, axis=(0, 1))

    start = jnp.zeros((BLK_GRP, N_MM, 3, ATOMS), jnp.float32)
    mm_force, tile_force = lax.scan(per_tile, start, (centers, widths, weight, pattern))
    return mm_force, tile_force
```

```python
import functools

import jax
import jax.numpy as jnp
from jax import lax
from jax.experimental import pallas as pl
from jax.experimental.pallas import tpu as pltpu
from jax.sharding import PartitionSpec as P

ROWS = 16


def pair_kernel(
    pattern_ref, padding_ref, pkg_ref, atoms_ref, mm_ref, tile_ref, cols, near_atoms, acc, tsum
):
    tiles, _, pairs = pkg_ref.shape
    near = pattern_ref.shape[0] // tiles
    mm_ref[...] = jnp.zeros_like(mm_ref)

    def one_tile(t, carry):
        cols[:, 0:8] = pkg_ref[t].T
        tsum[...] = jnp.zeros_like(tsum)
        for n in range(near):
            b = pattern_ref[t * near + n]
            for i in range(4):
                near_atoms[n, i] = jnp.broadcast_to(atoms_ref[b, i : i + 1, :], (8, 128))
            for i in range(3):
                acc[n, i] = jnp.zeros((8, 128), jnp.float32)
        steps = (pairs - padding_ref[t] + ROWS - 1) // ROWS

        def one_step(j, carry):
            row = pl.multiple_of(j * ROWS, ROWS)
            groups = []
            for h in range(ROWS // 8):
                col = cols[pl.ds(row + 8 * h, 8), :]
                groups.append(
                    [jnp.broadcast_to(col[:, i : i + 1], (8, 128)) for i in range(5)]
                )
            total = [[None] * 3 for _ in groups]
            for n in range(near):
                x, y, z, q = (near_atoms[n, i] for i in range(4))
                here = [None] * 3
                for h, (cx, cy, cz, wid, wgt) in enumerate(groups):
                    dx, dy, dz = x - cx, y - cy, z - cz
                    s = (dx * dx + dy * dy) + (dz * dz + wid)
                    r = lax.rsqrt(s)
                    coef = (wgt * q) * (r * r * r)
                    for i, d in enumerate((dx, dy, dz)):
                        f = coef * d
                        here[i] = f if here[i] is None else here[i] + f
                        total[h][i] = f if total[h][i] is None else total[h][i] + f
                for i in range(3):
                    acc[n, i] += here[i]
            for h in range(len(groups)):
                for i in range(3):
                    tsum[pl.ds(row + 8 * h, 8), i : i + 1] = -jnp.sum(
                        total[h][i], axis=1, keepdims=True
                    )
            return carry

        lax.fori_loop(0, steps, one_step, 0)
        tile_ref[t] = tsum[:, 0:8].T
        for n in range(near):
            b = pattern_ref[t * near + n]
            rows = [jnp.sum(acc[n, i], axis=0, keepdims=True) for i in range(3)]
            for i in range(3):
                mm_ref[b, i : i + 1, :] += rows[i]
        return carry

    lax.fori_loop(0, tiles, one_tile, 0)


def interactions(blocks, padding, package, atoms):
    tiles, _, pairs = package.shape
    near = blocks.shape[0] // tiles
    vmem = pl.BlockSpec(memory_space=pltpu.VMEM)
    smem = pl.BlockSpec(memory_space=pltpu.SMEM)
    return pl.pallas_call(
        pair_kernel,
        out_shape=(
            jax.ShapeDtypeStruct((atoms.shape[0], 3, atoms.shape[2]), jnp.float32),
            jax.ShapeDtypeStruct((tiles, 8, pairs), jnp.float32),
        ),
        in_specs=[smem, smem, vmem, vmem],
        out_specs=(vmem, vmem),
        scratch_shapes=[
            pltpu.VMEM((pairs, 128), jnp.float32),
            pltpu.VMEM((near, 4, 8, 128), jnp.float32),
            pltpu.VMEM((near, 3, 8, 128), jnp.float32),
            pltpu.VMEM((pairs, 128), jnp.float32),
        ],
        compiler_params=pltpu.CompilerParams(vmem_limit_bytes=48 * 1024 * 1024),
    )(blocks, padding, package, atoms)


def body(centers, widths, density, prefactor, padding, pattern, mm_coords, mm_charges):
    pairs = centers.shape[2]
    slots = jnp.arange(pairs, dtype=jnp.int32)[None, :]
    weight = jnp.where(slots < (pairs - padding)[:, None], density * prefactor, jnp.float32(0.0))
    package = jnp.concatenate(
        [centers, widths[:, None, :], weight[:, None, :], jnp.zeros_like(centers)], axis=1
    )
    blocks = pattern[:, 0, :].reshape(-1)
    atoms = jnp.concatenate([mm_coords[:, 0], mm_charges], axis=1)
    atoms = lax.all_gather(atoms, "pair", axis=0, tiled=True)
    mm_part, tile_part = interactions(blocks, padding, package, atoms)
    mm_part = lax.psum_scatter(mm_part, "pair", scatter_dimension=0, tiled=True)
    mm_force = lax.psum(mm_part, "sub")[:, None]
    tile_force = lax.psum(tile_part[:, 0:3], "mm")
    return (mm_force, tile_force)


def solution(mesh):
    tiles = P(("groups", "pair", "sub"))
    placed = (
        tiles,
        tiles,
        tiles,
        tiles,
        tiles,
        P(("groups", "pair", "sub"), "mm", None),
        P(("groups", "pair"), "mm", None, None),
        P(("groups", "pair"), "mm", None),
    )
    return jax.shard_map(
        body,
        mesh=mesh,
        in_specs=placed,
        out_specs=(P(("groups", "pair"), "mm", None, None), tiles),
        check_vma=False,
    )
```

```python
import functools

import jax
import jax.numpy as jnp
from jax import lax
from jax.experimental import pallas as pl
from jax.experimental.pallas import tpu as pltpu
from jax.sharding import PartitionSpec as P

ROWS = 16
LIMIT = 48 * 1024 * 1024
VMEM = pl.BlockSpec(memory_space=pltpu.VMEM)
SMEM = pl.BlockSpec(memory_space=pltpu.SMEM)


def remote(src, dst, send, recv, **where):
    return pltpu.make_async_remote_copy(
        src_ref=src,
        dst_ref=dst,
        send_sem=send,
        recv_sem=recv,
        device_id=where,
        device_id_type=pl.DeviceIdType.MESH,
    )


def greet(peers):
    barrier = pltpu.get_barrier_semaphore()
    for where in peers:
        pl.semaphore_signal(
            barrier, inc=1, device_id=where, device_id_type=pl.DeviceIdType.MESH
        )
    pl.semaphore_wait(barrier, len(peers))


def gather_kernel(n, coords_ref, charges_ref, out_ref, send, recv, core_send, core_recv):
    owned = coords_ref.shape[0]
    half = owned // 2
    p, s = lax.axis_index("pair"), lax.axis_index("sub")
    mine = pl.multiple_of(p * owned, owned)
    out_ref[pl.ds(mine, owned), 0:3, :] = coords_ref[:, 0]
    out_ref[pl.ds(mine, owned), 3:4, :] = charges_ref[...]
    peers = [lax.rem(p + k, n) for k in range(1, n)]
    greet([{"pair": q} for q in peers] + [{"sub": 1 - s}])

    def part(q):
        return out_ref.at[pl.ds(pl.multiple_of(q * owned + s * half, half), half)]

    out = [
        remote(part(p), part(p), send.at[k], recv.at[k], pair=q) for k, q in enumerate(peers)
    ]
    for copy in out:
        copy.start()
    across = []
    for k in range(n - 1):
        out[k].wait_recv()
        q = lax.rem(p + n - 1 - k, n)
        copy = remote(part(q), part(q), core_send.at[k], core_recv.at[k], sub=1 - s)
        copy.start()
        across.append(copy)
    for copy in across:
        copy.wait()
    for copy in out:
        copy.wait_send()


def gather(n, coords, charges):
    owned, _, _, atoms = coords.shape
    return pl.pallas_call(
        functools.partial(gather_kernel, n),
        out_shape=jax.ShapeDtypeStruct((n * owned, 4, atoms), jnp.float32),
        in_specs=[VMEM] * 2,
        out_specs=VMEM,
        scratch_shapes=[pltpu.SemaphoreType.DMA((n - 1,))] * 4,
        compiler_params=pltpu.CompilerParams(
            collective_id=0, has_side_effects=True, vmem_limit_bytes=LIMIT
        ),
    )(coords, charges)


def reduce_kernel(
    n,
    groups,
    part_ref,
    tile_ref,
    mm_ref,
    sum_ref,
    swapped,
    summed,
    landed,
    tile_landed,
    core_send,
    core_recv,
    send,
    recv,
    tile_send,
    tile_recv,
    last_send,
    last_recv,
):
    p, m, s = (lax.axis_index(a) for a in ("pair", "mm", "sub"))
    peers = [lax.rem(p + k, n) for k in range(1, n)] + [p]
    others = [lax.rem(m + k, groups) for k in range(1, groups)]
    greet([{"pair": q} for q in peers[:-1]] + [{"sub": 1 - s}] + [{"mm": g} for g in others])
    across = [
        remote(part_ref.at[q, 1 - s], swapped.at[k], core_send.at[k], core_recv.at[k], sub=1 - s)
        for k, q in enumerate(peers)
    ]
    for copy in across:
        copy.start()
    tiles = [
        remote(tile_ref, tile_landed.at[k], tile_send.at[k], tile_recv.at[k], mm=g)
        for k, g in enumerate(others)
    ]
    for copy in tiles:
        copy.start()
    out = []
    for k, q in enumerate(peers):
        across[k].wait_recv()
        if k < n - 1:
            summed[k] = part_ref[q, s] + swapped[k]
            copy = remote(summed.at[k], landed.at[k], send.at[k], recv.at[k], pair=q)
            copy.start()
            out.append(copy)
        else:
            total = part_ref[q, s] + swapped[k]
    for k, copy in enumerate(out):
        copy.wait_recv()
        total = total + landed[k]
    mm_ref[s] = total
    last = remote(mm_ref.at[s], mm_ref.at[s], last_send.at[0], last_recv.at[0], sub=1 - s)
    last.start()
    tile_total = tile_ref[...]
    for k, copy in enumerate(tiles):
        copy.wait_recv()
        tile_total = tile_total + tile_landed[k]
    sum_ref[...] = tile_total
    last.wait()
    for copy in across + out + tiles:
        copy.wait_send()


def reduce(n, groups, mm_part, tile_part):
    piece = mm_part.shape[2:]
    dma = pltpu.SemaphoreType.DMA
    return pl.pallas_call(
        functools.partial(reduce_kernel, n, groups),
        out_shape=(
            jax.ShapeDtypeStruct((2,) + piece, jnp.float32),
            jax.ShapeDtypeStruct(tile_part.shape, jnp.float32),
        ),
        in_specs=[VMEM] * 2,
        out_specs=(VMEM, VMEM),
        scratch_shapes=[
            pltpu.VMEM((n,) + piece, jnp.float32),
            pltpu.VMEM((n - 1,) + piece, jnp.float32),
            pltpu.VMEM((n - 1,) + piece, jnp.float32),
            pltpu.VMEM((groups - 1,) + tile_part.shape, jnp.float32),
            dma((n,)),
            dma((n,)),
            dma((n - 1,)),
            dma((n - 1,)),
            dma((groups - 1,)),
            dma((groups - 1,)),
            dma((1,)),
            dma((1,)),
        ],
        compiler_params=pltpu.CompilerParams(
            collective_id=1, has_side_effects=True, vmem_limit_bytes=LIMIT
        ),
    )(mm_part, tile_part)


def pair_kernel(
    pattern_ref,
    padding_ref,
    centers_ref,
    widths_ref,
    density_ref,
    prefactor_ref,
    atoms_ref,
    mm_ref,
    tile_ref,
    rows_scr,
    cols,
    near_atoms,
    acc,
    tsum,
):
    tiles, _, pairs = centers_ref.shape
    near = pattern_ref.shape[2]
    half = mm_ref.shape[1]
    mm_ref[...] = jnp.zeros_like(mm_ref)
    rows_scr[...] = jnp.zeros_like(rows_scr)
    slots = lax.broadcasted_iota(jnp.int32, (1, pairs), 1)

    def one_tile(t, carry):
        valid = pairs - padding_ref[t]
        rows_scr[0:3, :] = centers_ref[t]
        rows_scr[3:4, :] = widths_ref[pl.ds(t, 1), :]
        rows_scr[4:5, :] = jnp.where(
            slots < valid, density_ref[pl.ds(t, 1), :] * prefactor_ref[pl.ds(t, 1), :], 0.0
        )
        cols[:, 0:8] = rows_scr[...].T
        tsum[...] = jnp.zeros_like(tsum)
        for n in range(near):
            b = pattern_ref[t, 0, n]
            for i in range(4):
                near_atoms[n, i] = jnp.broadcast_to(atoms_ref[b, i : i + 1, :], (8, 128))
            for i in range(3):
                acc[n, i] = jnp.zeros((8, 128), jnp.float32)
        steps = lax.div(valid + ROWS - 1, ROWS)

        def one_step(j, carry):
            row = pl.multiple_of(j * ROWS, ROWS)
            groups = []
            for h in range(ROWS // 8):
                col = cols[pl.ds(row + 8 * h, 8), :]
                groups.append(
                    [jnp.broadcast_to(col[:, i : i + 1], (8, 128)) for i in range(5)]
                )
            total = [[None] * 3 for _ in groups]
            for n in range(near):
                x, y, z, q = (near_atoms[n, i] for i in range(4))
                here = [None] * 3
                for h, (cx, cy, cz, wid, wgt) in enumerate(groups):
                    dx, dy, dz = x - cx, y - cy, z - cz
                    s = (dx * dx + dy * dy) + (dz * dz + wid)
                    r = lax.rsqrt(s)
                    coef = (wgt * q) * (r * r * r)
                    for i, d in enumerate((dx, dy, dz)):
                        f = coef * d
                        here[i] = f if here[i] is None else here[i] + f
                        total[h][i] = f if total[h][i] is None else total[h][i] + f
                for i in range(3):
                    acc[n, i] += here[i]
            for h in range(len(groups)):
                for i in range(3):
                    tsum[pl.ds(row + 8 * h, 8), i : i + 1] = -jnp.sum(
                        total[h][i], axis=1, keepdims=True
                    )
            return carry

        lax.fori_loop(0, steps, one_step, 0)
        forces = tsum[:, 0:8].T
        for i in range(3):
            tile_ref[i, pl.ds(t, 1), :] = forces[i : i + 1, :]
        for n in range(near):
            b = pattern_ref[t, 0, n]
            piece = lax.div(b, half)
            row = b - piece * half
            for i in range(3):
                mm_ref[piece * 3 + i, pl.ds(row, 1), :] += jnp.sum(
                    acc[n, i], axis=0, keepdims=True
                )
        return carry

    lax.fori_loop(0, tiles, one_tile, 0)


def interactions(half, pattern, padding, centers, widths, density, prefactor, atoms):
    tiles, _, pairs = centers.shape
    near = pattern.shape[2]
    return pl.pallas_call(
        pair_kernel,
        out_shape=(
            jax.ShapeDtypeStruct((atoms.shape[0] // half * 3, half, 128), jnp.float32),
            jax.ShapeDtypeStruct((3, tiles, pairs), jnp.float32),
        ),
        in_specs=[SMEM] * 2 + [VMEM] * 5,
        out_specs=(VMEM, VMEM),
        scratch_shapes=[
            pltpu.VMEM((8, pairs), jnp.float32),
            pltpu.VMEM((pairs, 128), jnp.float32),
            pltpu.VMEM((near, 4, 8, 128), jnp.float32),
            pltpu.VMEM((near, 3, 8, 128), jnp.float32),
            pltpu.VMEM((pairs, 128), jnp.float32),
        ],
        compiler_params=pltpu.CompilerParams(vmem_limit_bytes=LIMIT),
    )(pattern, padding, centers, widths, density, prefactor, atoms)


def body(n, groups, centers, widths, density, prefactor, padding, pattern, mm_coords, mm_charges):
    owned = mm_coords.shape[0]
    half = owned // 2
    atoms = gather(n, mm_coords, mm_charges)
    mm_part, tile_part = interactions(
        half, pattern, padding, centers, widths, density, prefactor, atoms
    )
    mm_part = mm_part.reshape(n, 2, 3, half, mm_coords.shape[3])
    mm_force, tile_force = reduce(n, groups, mm_part, tile_part)
    mm_force = mm_force.transpose(0, 2, 1, 3).reshape(mm_coords.shape)
    return (mm_force, tile_force.transpose(1, 0, 2))


def solution(mesh):
    tiles = P(("groups", "pair", "sub"))
    placed = (
        tiles,
        tiles,
        tiles,
        tiles,
        tiles,
        P(("groups", "pair", "sub"), "mm", None),
        P(("groups", "pair"), "mm", None, None),
        P(("groups", "pair"), "mm", None),
    )
    return jax.shard_map(
        functools.partial(body, mesh.shape["pair"], mesh.shape["mm"]),
        mesh=mesh,
        in_specs=placed,
        out_specs=(P(("groups", "pair"), "mm", None, None), tiles),
        check_vma=False,
    )
```

```python
import functools

import jax
import jax.numpy as jnp
from jax import lax
from jax.experimental import pallas as pl
from jax.experimental.pallas import tpu as pltpu
from jax.sharding import PartitionSpec as P

ROWS = 16
LIMIT = 48 * 1024 * 1024
VMEM = pl.BlockSpec(memory_space=pltpu.VMEM)
SMEM = pl.BlockSpec(memory_space=pltpu.SMEM)


def remote(src, dst, send, recv, **where):
    return pltpu.make_async_remote_copy(
        src_ref=src,
        dst_ref=dst,
        send_sem=send,
        recv_sem=recv,
        device_id=where,
        device_id_type=pl.DeviceIdType.MESH,
    )


def greet(peers):
    barrier = pltpu.get_barrier_semaphore()
    for where in peers:
        pl.semaphore_signal(
            barrier, inc=1, device_id=where, device_id_type=pl.DeviceIdType.MESH
        )
    pl.semaphore_wait(barrier, len(peers))


def gather_kernel(n, coords_ref, charges_ref, out_ref, send, recv, core_send, core_recv):
    owned = coords_ref.shape[0]
    half = owned // 2
    p, s = lax.axis_index("pair"), lax.axis_index("sub")
    mine = pl.multiple_of(p * owned, owned)
    out_ref[pl.ds(mine, owned), 0:3, :] = coords_ref[:, 0]
    out_ref[pl.ds(mine, owned), 3:4, :] = charges_ref[...]
    peers = [lax.rem(p + k, n) for k in range(1, n)]
    greet([{"pair": q} for q in peers] + [{"sub": 1 - s}])

    def part(q):
        return out_ref.at[pl.ds(pl.multiple_of(q * owned + s * half, half), half)]

    out = [
        remote(part(p), part(p), send.at[k], recv.at[k], pair=q) for k, q in enumerate(peers)
    ]
    for copy in out:
        copy.start()
    across = []
    for k in range(n - 1):
        out[k].wait_recv()
        q = lax.rem(p + n - 1 - k, n)
        copy = remote(part(q), part(q), core_send.at[k], core_recv.at[k], sub=1 - s)
        copy.start()
        across.append(copy)
    for copy in across:
        copy.wait()
    for copy in out:
        copy.wait_send()


def gather(n, coords, charges):
    owned, _, _, atoms = coords.shape
    return pl.pallas_call(
        functools.partial(gather_kernel, n),
        out_shape=jax.ShapeDtypeStruct((n * owned, 4, atoms), jnp.float32),
        in_specs=[VMEM] * 2,
        out_specs=VMEM,
        scratch_shapes=[pltpu.SemaphoreType.DMA((n - 1,))] * 4,
        compiler_params=pltpu.CompilerParams(
            collective_id=0, has_side_effects=True, vmem_limit_bytes=LIMIT
        ),
    )(coords, charges)


def reduce_kernel(
    n,
    groups,
    part_ref,
    tile_ref,
    mm_ref,
    sum_ref,
    swapped,
    summed,
    landed,
    tile_landed,
    core_send,
    core_recv,
    send,
    recv,
    tile_send,
    tile_recv,
    last_send,
    last_recv,
):
    p, m, s = (lax.axis_index(a) for a in ("pair", "mm", "sub"))
    peers = [lax.rem(p + k, n) for k in range(1, n)] + [p]
    others = [lax.rem(m + k, groups) for k in range(1, groups)]
    greet([{"pair": q} for q in peers[:-1]] + [{"sub": 1 - s}] + [{"mm": g} for g in others])
    across = [
        remote(part_ref.at[q, 1 - s], swapped.at[k], core_send.at[k], core_recv.at[k], sub=1 - s)
        for k, q in enumerate(peers)
    ]
    for copy in across:
        copy.start()
    tiles = [
        remote(tile_ref, tile_landed.at[k], tile_send.at[k], tile_recv.at[k], mm=g)
        for k, g in enumerate(others)
    ]
    for copy in tiles:
        copy.start()
    out = []
    for k, q in enumerate(peers):
        across[k].wait_recv()
        if k < n - 1:
            summed[k] = part_ref[q, s] + swapped[k]
            copy = remote(summed.at[k], landed.at[k], send.at[k], recv.at[k], pair=q)
            copy.start()
            out.append(copy)
        else:
            total = part_ref[q, s] + swapped[k]
    for k, copy in enumerate(out):
        copy.wait_recv()
        total = total + landed[k]
    mm_ref[s] = total
    last = remote(mm_ref.at[s], mm_ref.at[s], last_send.at[0], last_recv.at[0], sub=1 - s)
    last.start()
    tile_total = tile_ref[...]
    for k, copy in enumerate(tiles):
        copy.wait_recv()
        tile_total = tile_total + tile_landed[k]
    sum_ref[...] = tile_total
    last.wait()
    for copy in across + out + tiles:
        copy.wait_send()


def reduce(n, groups, mm_part, tile_part):
    piece = mm_part.shape[2:]
    dma = pltpu.SemaphoreType.DMA
    return pl.pallas_call(
        functools.partial(reduce_kernel, n, groups),
        out_shape=(
            jax.ShapeDtypeStruct((2,) + piece, jnp.float32),
            jax.ShapeDtypeStruct(tile_part.shape, jnp.float32),
        ),
        in_specs=[VMEM] * 2,
        out_specs=(VMEM, VMEM),
        scratch_shapes=[
            pltpu.VMEM((n,) + piece, jnp.float32),
            pltpu.VMEM((n - 1,) + piece, jnp.float32),
            pltpu.VMEM((n - 1,) + piece, jnp.float32),
            pltpu.VMEM((groups - 1,) + tile_part.shape, jnp.float32),
            dma((n,)),
            dma((n,)),
            dma((n - 1,)),
            dma((n - 1,)),
            dma((groups - 1,)),
            dma((groups - 1,)),
            dma((1,)),
            dma((1,)),
        ],
        compiler_params=pltpu.CompilerParams(
            collective_id=1, has_side_effects=True, vmem_limit_bytes=LIMIT
        ),
    )(mm_part, tile_part)


def pair_kernel(
    pattern_ref,
    padding_ref,
    centers_ref,
    widths_ref,
    density_ref,
    prefactor_ref,
    atoms_ref,
    mm_ref,
    tile_ref,
    wide,
    near_atoms,
    acc,
    total,
):
    tiles, _, pairs = centers_ref.shape
    near = pattern_ref.shape[2]
    half = mm_ref.shape[1]
    mm_ref[...] = jnp.zeros_like(mm_ref)
    slots = lax.broadcasted_iota(jnp.int32, (1, pairs), 1)
    part = lax.broadcasted_iota(jnp.int32, (32, 5 * 128), 0)
    column = lax.broadcasted_iota(jnp.int32, (32, 5 * 128), 1)
    spread = jnp.where(
        (part < 24) & ((part & 7) == (column >> 7)), 1.0, 0.0
    ).astype(jnp.bfloat16)
    for t in range(tiles):
        weight = jnp.where(
            slots < pairs - padding_ref[t],
            density_ref[t : t + 1, :] * prefactor_ref[t : t + 1, :],
            0.0,
        )
        rest = jnp.concatenate(
            [centers_ref[t], widths_ref[t : t + 1, :], weight, jnp.zeros((3, pairs), jnp.float32)],
            axis=0,
        )
        pieces = []
        for _ in range(3):
            piece = rest.astype(jnp.bfloat16).astype(jnp.float32)
            pieces.append(piece)
            rest = rest - piece
        pieces.append(jnp.zeros_like(rest))
        pieces = jnp.concatenate(pieces, axis=0).astype(jnp.bfloat16)
        over = lax.dot_general(
            pieces, spread, (((0,), (0,)), ((), ())), preferred_element_type=jnp.float32
        )
        for i in range(5):
            wide[t, i] = over[:, 128 * i : 128 * (i + 1)]

    def one_tile(t, carry):
        valid = pairs - padding_ref[t]
        for n in range(near):
            b = pattern_ref[t, 0, n]
            for i in range(4):
                near_atoms[n, i] = jnp.broadcast_to(atoms_ref[b, i : i + 1, :], (8, 128))
            for i in range(3):
                acc[n, i] = jnp.zeros((8, 128), jnp.float32)
        steps = lax.div(valid + ROWS - 1, ROWS)

        def one_step(j, carry):
            row = pl.multiple_of(j * ROWS, ROWS)
            groups = [
                [wide[t, i, pl.ds(row + 8 * h, 8), :] for i in range(5)]
                for h in range(ROWS // 8)
            ]
            sums = [[None] * 3 for _ in groups]
            for n in range(near):
                x, y, z, q = (near_atoms[n, i] for i in range(4))
                here = [None] * 3
                for h, (cx, cy, cz, wid, wgt) in enumerate(groups):
                    dx, dy, dz = x - cx, y - cy, z - cz
                    s = (dx * dx + dy * dy) + (dz * dz + wid)
                    r = lax.rsqrt(s)
                    coef = (wgt * q) * (r * r * r)
                    for i, d in enumerate((dx, dy, dz)):
                        f = coef * d
                        here[i] = f if here[i] is None else here[i] + f
                        sums[h][i] = f if sums[h][i] is None else sums[h][i] + f
                for i in range(3):
                    acc[n, i] += here[i]
            for h in range(len(groups)):
                for i in range(3):
                    total[t, i, pl.ds(row + 8 * h, 8), :] = sums[h][i]
            return carry

        lax.fori_loop(0, steps, one_step, 0)
        for n in range(near):
            b = pattern_ref[t, 0, n]
            piece = lax.div(b, half)
            row = b - piece * half
            for i in range(3):
                mm_ref[piece * 3 + i, pl.ds(row, 1), :] += jnp.sum(
                    acc[n, i], axis=0, keepdims=True
                )
        return carry

    lax.fori_loop(0, tiles, one_tile, 0)
    ones = jnp.ones((16, 2 * 128), jnp.bfloat16)
    for t in range(tiles):
        for i in range(3):
            whole = total[t, i]
            high = whole.astype(jnp.bfloat16)
            low = (whole - high.astype(jnp.float32)).astype(jnp.bfloat16)
            line = lax.dot_general(
                ones,
                jnp.concatenate([high, low], axis=1),
                (((1,), (1,)), ((), ())),
                preferred_element_type=jnp.float32,
            )
            tile_ref[i, t : t + 1, :] = jnp.where(
                slots < pairs - padding_ref[t], -line[0:1, :], 0.0
            )


def interactions(half, pattern, padding, centers, widths, density, prefactor, atoms):
    tiles, _, pairs = centers.shape
    near = pattern.shape[2]
    return pl.pallas_call(
        pair_kernel,
        out_shape=(
            jax.ShapeDtypeStruct((atoms.shape[0] // half * 3, half, 128), jnp.float32),
            jax.ShapeDtypeStruct((3, tiles, pairs), jnp.float32),
        ),
        in_specs=[SMEM] * 2 + [VMEM] * 5,
        out_specs=(VMEM, VMEM),
        scratch_shapes=[
            pltpu.VMEM((tiles, 5, pairs, 128), jnp.float32),
            pltpu.VMEM((near, 4, 8, 128), jnp.float32),
            pltpu.VMEM((near, 3, 8, 128), jnp.float32),
            pltpu.VMEM((tiles, 3, pairs, 128), jnp.float32),
        ],
        compiler_params=pltpu.CompilerParams(vmem_limit_bytes=LIMIT),
    )(pattern, padding, centers, widths, density, prefactor, atoms)


def body(n, groups, centers, widths, density, prefactor, padding, pattern, mm_coords, mm_charges):
    owned = mm_coords.shape[0]
    half = owned // 2
    atoms = gather(n, mm_coords, mm_charges)
    mm_part, tile_part = interactions(
        half, pattern, padding, centers, widths, density, prefactor, atoms
    )
    mm_part = mm_part.reshape(n, 2, 3, half, mm_coords.shape[3])
    mm_force, tile_force = reduce(n, groups, mm_part, tile_part)
    mm_force = mm_force.transpose(0, 2, 1, 3).reshape(mm_coords.shape)
    return (mm_force, tile_force.transpose(1, 0, 2))


def solution(mesh):
    tiles = P(("groups", "pair", "sub"))
    placed = (
        tiles,
        tiles,
        tiles,
        tiles,
        tiles,
        P(("groups", "pair", "sub"), "mm", None),
        P(("groups", "pair"), "mm", None, None),
        P(("groups", "pair"), "mm", None),
    )
    return jax.shard_map(
        functools.partial(body, mesh.shape["pair"], mesh.shape["mm"]),
        mesh=mesh,
        in_specs=placed,
        out_specs=(P(("groups", "pair"), "mm", None, None), tiles),
        check_vma=False,
    )
```

```python
import functools

import jax
import jax.numpy as jnp
from jax import lax
from jax.experimental import pallas as pl
from jax.experimental.pallas import tpu as pltpu
from jax.sharding import PartitionSpec as P

ROWS = 16
LIMIT = 48 * 1024 * 1024
VMEM = pl.BlockSpec(memory_space=pltpu.VMEM)
SMEM = pl.BlockSpec(memory_space=pltpu.SMEM)


def remote(src, dst, send, recv, **where):
    return pltpu.make_async_remote_copy(
        src_ref=src,
        dst_ref=dst,
        send_sem=send,
        recv_sem=recv,
        device_id=where,
        device_id_type=pl.DeviceIdType.MESH,
    )


def greet(peers):
    barrier = pltpu.get_barrier_semaphore()
    for where in peers:
        pl.semaphore_signal(
            barrier, inc=1, device_id=where, device_id_type=pl.DeviceIdType.MESH
        )
    pl.semaphore_wait(barrier, len(peers))


def gather_kernel(n, coords_ref, charges_ref, out_ref, send, recv, core_send, core_recv):
    first = coords_ref.shape[0]
    owned = first + charges_ref.shape[0]
    half = owned // 2
    p, s = lax.axis_index("pair"), lax.axis_index("sub")
    mine = pl.multiple_of(p * owned, owned)
    out_ref[pl.ds(mine, first), :] = coords_ref[...]
    out_ref[pl.ds(mine + first, owned - first), :] = charges_ref[...]
    peers = [lax.rem(p + k, n) for k in range(1, n)]
    greet([{"pair": q} for q in peers] + [{"sub": 1 - s}])

    def part(q):
        return out_ref.at[pl.ds(pl.multiple_of(q * owned + s * half, half), half)]

    out = [
        remote(part(p), part(p), send.at[k], recv.at[k], pair=q) for k, q in enumerate(peers)
    ]
    for copy in out:
        copy.start()
    across = []
    for k in range(n - 1):
        out[k].wait_recv()
        q = lax.rem(p + n - 1 - k, n)
        copy = remote(part(q), part(q), core_send.at[k], core_recv.at[k], sub=1 - s)
        copy.start()
        across.append(copy)
    for copy in across:
        copy.wait()
    for copy in out:
        copy.wait_send()


def gather(n, coords, charges):
    rows = coords.shape[0] + charges.shape[0]
    return pl.pallas_call(
        functools.partial(gather_kernel, n),
        out_shape=jax.ShapeDtypeStruct((n * rows, coords.shape[1]), jnp.float32),
        in_specs=[VMEM] * 2,
        out_specs=VMEM,
        scratch_shapes=[pltpu.SemaphoreType.DMA((n - 1,))] * 4,
        compiler_params=pltpu.CompilerParams(
            collective_id=0, has_side_effects=True, vmem_limit_bytes=LIMIT
        ),
    )(coords, charges)


def reduce_kernel(
    n,
    groups,
    part_ref,
    tile_ref,
    mm_ref,
    sum_ref,
    swapped,
    summed,
    landed,
    tile_landed,
    core_send,
    core_recv,
    send,
    recv,
    tile_send,
    tile_recv,
    last_send,
    last_recv,
):
    p, m, s = (lax.axis_index(a) for a in ("pair", "mm", "sub"))
    peers = [lax.rem(p + k, n) for k in range(1, n)] + [p]
    others = [lax.rem(m + k, groups) for k in range(1, groups)]
    greet([{"pair": q} for q in peers[:-1]] + [{"sub": 1 - s}] + [{"mm": g} for g in others])
    across = [
        remote(part_ref.at[q, 1 - s], swapped.at[k], core_send.at[k], core_recv.at[k], sub=1 - s)
        for k, q in enumerate(peers)
    ]
    for copy in across:
        copy.start()
    tiles = [
        remote(tile_ref, tile_landed.at[k], tile_send.at[k], tile_recv.at[k], mm=g)
        for k, g in enumerate(others)
    ]
    for copy in tiles:
        copy.start()
    out = []
    for k, q in enumerate(peers):
        across[k].wait_recv()
        if k < n - 1:
            summed[k] = part_ref[q, s] + swapped[k]
            copy = remote(summed.at[k], landed.at[k], send.at[k], recv.at[k], pair=q)
            copy.start()
            out.append(copy)
        else:
            total = part_ref[q, s] + swapped[k]
    for k, copy in enumerate(out):
        copy.wait_recv()
        total = total + landed[k]
    mm_ref[s] = total
    last = remote(mm_ref.at[s], mm_ref.at[s], last_send.at[0], last_recv.at[0], sub=1 - s)
    last.start()
    tile_total = tile_ref[...]
    for k, copy in enumerate(tiles):
        copy.wait_recv()
        tile_total = tile_total + tile_landed[k]
    sum_ref[...] = tile_total
    last.wait()
    for copy in across + out + tiles:
        copy.wait_send()


def reduce(n, groups, mm_part, tile_part):
    piece = mm_part.shape[2:]
    dma = pltpu.SemaphoreType.DMA
    return pl.pallas_call(
        functools.partial(reduce_kernel, n, groups),
        out_shape=(
            jax.ShapeDtypeStruct((2,) + piece, jnp.float32),
            jax.ShapeDtypeStruct(tile_part.shape, jnp.float32),
        ),
        in_specs=[VMEM] * 2,
        out_specs=(VMEM, VMEM),
        scratch_shapes=[
            pltpu.VMEM((n,) + piece, jnp.float32),
            pltpu.VMEM((n - 1,) + piece, jnp.float32),
            pltpu.VMEM((n - 1,) + piece, jnp.float32),
            pltpu.VMEM((groups - 1,) + tile_part.shape, jnp.float32),
            dma((n,)),
            dma((n,)),
            dma((n - 1,)),
            dma((n - 1,)),
            dma((groups - 1,)),
            dma((groups - 1,)),
            dma((1,)),
            dma((1,)),
        ],
        compiler_params=pltpu.CompilerParams(
            collective_id=1, has_side_effects=True, vmem_limit_bytes=LIMIT
        ),
    )(mm_part, tile_part)


def pair_kernel(
    owned,
    pattern_ref,
    padding_ref,
    centers_ref,
    widths_ref,
    density_ref,
    prefactor_ref,
    atoms_ref,
    mm_ref,
    tile_ref,
    wide,
    near_atoms,
    acc,
    total,
):
    _, tiles, pairs = centers_ref.shape
    near = pattern_ref.shape[2]
    mm_ref[...] = jnp.zeros_like(mm_ref)
    slots = lax.broadcasted_iota(jnp.int32, (1, pairs), 1)
    part = lax.broadcasted_iota(jnp.int32, (32, 5 * 128), 0)
    column = lax.broadcasted_iota(jnp.int32, (32, 5 * 128), 1)
    spread = jnp.where(
        (part < 24) & ((part & 7) == (column >> 7)), 1.0, 0.0
    ).astype(jnp.bfloat16)
    for t in range(tiles):
        weight = jnp.where(
            slots < pairs - padding_ref[t],
            density_ref[t : t + 1, :] * prefactor_ref[t : t + 1, :],
            0.0,
        )
        rest = jnp.concatenate(
            [centers_ref[i, t : t + 1, :] for i in range(3)]
            + [widths_ref[t : t + 1, :], weight, jnp.zeros((3, pairs), jnp.float32)],
            axis=0,
        )
        pieces = []
        for _ in range(3):
            piece = rest.astype(jnp.bfloat16).astype(jnp.float32)
            pieces.append(piece)
            rest = rest - piece
        pieces.append(jnp.zeros_like(rest))
        pieces = jnp.concatenate(pieces, axis=0).astype(jnp.bfloat16)
        over = lax.dot_general(
            pieces, spread, (((0,), (0,)), ((), ())), preferred_element_type=jnp.float32
        )
        for i in range(5):
            wide[t, i] = over[:, 128 * i : 128 * (i + 1)]

    def one_tile(t, carry):
        valid = pairs - padding_ref[t]
        for n in range(near):
            b = pattern_ref[t, 0, n]
            shard = lax.div(b, owned)
            for i in range(3):
                row = b * 3 + shard * owned + i
                near_atoms[n, i] = jnp.broadcast_to(atoms_ref[pl.ds(row, 1), :], (8, 128))
            row = b + (shard + 1) * (3 * owned)
            near_atoms[n, 3] = jnp.broadcast_to(atoms_ref[pl.ds(row, 1), :], (8, 128))
            for i in range(3):
                acc[n, i] = jnp.zeros((8, 128), jnp.float32)
        steps = lax.div(valid + ROWS - 1, ROWS)

        def one_step(j, carry):
            row = pl.multiple_of(j * ROWS, ROWS)
            groups = [
                [wide[t, i, pl.ds(row + 8 * h, 8), :] for i in range(5)]
                for h in range(ROWS // 8)
            ]
            sums = [[None] * 3 for _ in groups]
            for n in range(near):
                x, y, z, q = (near_atoms[n, i] for i in range(4))
                here = [None] * 3
                for h, (cx, cy, cz, wid, wgt) in enumerate(groups):
                    dx, dy, dz = x - cx, y - cy, z - cz
                    s = (dx * dx + dy * dy) + (dz * dz + wid)
                    r = lax.rsqrt(s)
                    coef = (wgt * q) * (r * r * r)
                    for i, d in enumerate((dx, dy, dz)):
                        f = coef * d
                        here[i] = f if here[i] is None else here[i] + f
                        sums[h][i] = f if sums[h][i] is None else sums[h][i] + f
                for i in range(3):
                    acc[n, i] += here[i]
            for h in range(len(groups)):
                for i in range(3):
                    total[t, i, pl.ds(row + 8 * h, 8), :] = sums[h][i]
            return carry

        lax.fori_loop(0, steps, one_step, 0)
        for n in range(near):
            b = pattern_ref[t, 0, n]
            for i in range(3):
                mm_ref[pl.ds(b * 3 + i, 1), :] += jnp.sum(acc[n, i], axis=0, keepdims=True)
        return carry

    lax.fori_loop(0, tiles, one_tile, 0)
    ones = jnp.ones((16, 2 * 128), jnp.bfloat16)
    for t in range(tiles):
        for i in range(3):
            whole = total[t, i]
            high = whole.astype(jnp.bfloat16)
            low = (whole - high.astype(jnp.float32)).astype(jnp.bfloat16)
            line = lax.dot_general(
                ones,
                jnp.concatenate([high, low], axis=1),
                (((1,), (1,)), ((), ())),
                preferred_element_type=jnp.float32,
            )
            tile_ref[i, t : t + 1, :] = jnp.where(
                slots < pairs - padding_ref[t], -line[0:1, :], 0.0
            )


def interactions(owned, pattern, padding, centers, widths, density, prefactor, atoms):
    _, tiles, pairs = centers.shape
    near = pattern.shape[2]
    return pl.pallas_call(
        functools.partial(pair_kernel, owned),
        out_shape=(
            jax.ShapeDtypeStruct((atoms.shape[0] // 4 * 3, 128), jnp.float32),
            jax.ShapeDtypeStruct((3, tiles, pairs), jnp.float32),
        ),
        in_specs=[SMEM] * 2 + [VMEM] * 5,
        out_specs=(VMEM, VMEM),
        scratch_shapes=[
            pltpu.VMEM((tiles, 5, pairs, 128), jnp.float32),
            pltpu.VMEM((near, 4, 8, 128), jnp.float32),
            pltpu.VMEM((near, 3, 8, 128), jnp.float32),
            pltpu.VMEM((tiles, 3, pairs, 128), jnp.float32),
        ],
        compiler_params=pltpu.CompilerParams(vmem_limit_bytes=LIMIT),
    )(pattern, padding, centers, widths, density, prefactor, atoms)


def body(n, groups, centers, widths, density, prefactor, padding, pattern, mm_coords, mm_charges):
    owned, lanes = mm_coords.shape[0], mm_coords.shape[3]
    atoms = gather(n, mm_coords.reshape(3 * owned, lanes), mm_charges.reshape(owned, lanes))
    mm_part, tile_part = interactions(
        owned,
        pattern,
        padding,
        centers.transpose(1, 0, 2),
        widths,
        density,
        prefactor,
        atoms,
    )
    mm_part = mm_part.reshape(n, 2, 3 * owned // 2, lanes)
    mm_force, tile_force = reduce(n, groups, mm_part, tile_part)
    return (mm_force.reshape(mm_coords.shape), tile_force.transpose(1, 0, 2))


def solution(mesh):
    tiles = P(("groups", "pair", "sub"))
    placed = (
        tiles,
        tiles,
        tiles,
        tiles,
        tiles,
        P(("groups", "pair", "sub"), "mm", None),
        P(("groups", "pair"), "mm", None, None),
        P(("groups", "pair"), "mm", None),
    )
    return jax.shard_map(
        functools.partial(body, mesh.shape["pair"], mesh.shape["mm"]),
        mesh=mesh,
        in_specs=placed,
        out_specs=(P(("groups", "pair"), "mm", None, None), tiles),
        check_vma=False,
    )
```

```python
import functools

import jax
import jax.numpy as jnp
from jax import lax
from jax.experimental import pallas as pl
from jax.experimental.pallas import tpu as pltpu
from jax.sharding import PartitionSpec as P

ROWS = 16
LIMIT = 24 * 1024 * 1024
VMEM = pl.BlockSpec(memory_space=pltpu.VMEM)
SMEM = pl.BlockSpec(memory_space=pltpu.SMEM)


def remote(src, dst, send, recv, **where):
    return pltpu.make_async_remote_copy(
        src_ref=src,
        dst_ref=dst,
        send_sem=send,
        recv_sem=recv,
        device_id=where,
        device_id_type=pl.DeviceIdType.MESH,
    )


def greet(peers):
    barrier = pltpu.get_barrier_semaphore()
    for where in peers:
        pl.semaphore_signal(
            barrier, inc=1, device_id=where, device_id_type=pl.DeviceIdType.MESH
        )
    pl.semaphore_wait(barrier, len(peers))


def gather_kernel(n, shard_ref, out_ref, send, recv, core_send, core_recv):
    owned = shard_ref.shape[0]
    half = owned // 2
    p, s = lax.axis_index("pair"), lax.axis_index("sub")
    peers = [lax.rem(p + k, n) for k in range(1, n)]
    greet([{"pair": q} for q in peers] + [{"sub": 1 - s}])

    def part(q):
        return out_ref.at[pl.ds(pl.multiple_of(q * owned + s * half, half), half)]

    out = [
        remote(
            shard_ref.at[pl.ds(pl.multiple_of(s * half, half), half)],
            part(p),
            send.at[k],
            recv.at[k],
            pair=q,
        )
        for k, q in enumerate(peers)
    ]
    for copy in out:
        copy.start()
    out_ref[pl.ds(pl.multiple_of(p * owned, owned), owned), :] = shard_ref[...]
    across = []
    for k in range(n - 1):
        out[k].wait_recv()
        q = lax.rem(p + n - 1 - k, n)
        copy = remote(part(q), part(q), core_send.at[k], core_recv.at[k], sub=1 - s)
        copy.start()
        across.append(copy)
    for copy in across:
        copy.wait()
    for copy in out:
        copy.wait_send()


def gather(n, shard):
    return pl.pallas_call(
        functools.partial(gather_kernel, n),
        out_shape=jax.ShapeDtypeStruct((n * shard.shape[0], shard.shape[1]), jnp.float32),
        in_specs=[VMEM],
        out_specs=VMEM,
        scratch_shapes=[pltpu.SemaphoreType.DMA((n - 1,))] * 4,
        compiler_params=pltpu.CompilerParams(
            collective_id=0, has_side_effects=True, vmem_limit_bytes=LIMIT
        ),
    )(shard)


def reduce_kernel(
    n,
    groups,
    part_ref,
    tile_ref,
    mm_ref,
    sum_ref,
    swapped,
    summed,
    landed,
    tile_landed,
    core_send,
    core_recv,
    send,
    recv,
    tile_send,
    tile_recv,
    last_send,
    last_recv,
):
    p, m, s = (lax.axis_index(a) for a in ("pair", "mm", "sub"))
    peers = [lax.rem(p + k, n) for k in range(1, n)] + [p]
    others = [lax.rem(m + k, groups) for k in range(1, groups)]
    greet([{"pair": q} for q in peers[:-1]] + [{"sub": 1 - s}] + [{"mm": g} for g in others])
    across = [
        remote(part_ref.at[q, 1 - s], swapped.at[k], core_send.at[k], core_recv.at[k], sub=1 - s)
        for k, q in enumerate(peers)
    ]
    for copy in across:
        copy.start()
    tiles = [
        remote(tile_ref, tile_landed.at[k], tile_send.at[k], tile_recv.at[k], mm=g)
        for k, g in enumerate(others)
    ]
    for copy in tiles:
        copy.start()
    out = []
    for k, q in enumerate(peers):
        across[k].wait_recv()
        if k < n - 1:
            summed[k] = part_ref[q, s] + swapped[k]
            copy = remote(summed.at[k], landed.at[k], send.at[k], recv.at[k], pair=q)
            copy.start()
            out.append(copy)
        else:
            total = part_ref[q, s] + swapped[k]
    for k, copy in enumerate(out):
        copy.wait_recv()
        total = total + landed[k]
    mm_ref[s] = total
    last = remote(mm_ref.at[s], mm_ref.at[s], last_send.at[0], last_recv.at[0], sub=1 - s)
    last.start()
    tile_total = tile_ref[...]
    for k, copy in enumerate(tiles):
        copy.wait_recv()
        tile_total = tile_total + tile_landed[k]
    sum_ref[...] = tile_total
    last.wait()
    for copy in across + out + tiles:
        copy.wait_send()


def reduce(n, groups, mm_part, tile_part):
    piece = mm_part.shape[2:]
    dma = pltpu.SemaphoreType.DMA
    return pl.pallas_call(
        functools.partial(reduce_kernel, n, groups),
        out_shape=(
            jax.ShapeDtypeStruct((2,) + piece, jnp.float32),
            jax.ShapeDtypeStruct(tile_part.shape, jnp.float32),
        ),
        in_specs=[VMEM] * 2,
        out_specs=(VMEM, VMEM),
        scratch_shapes=[
            pltpu.VMEM((n,) + piece, jnp.float32),
            pltpu.VMEM((n - 1,) + piece, jnp.float32),
            pltpu.VMEM((n - 1,) + piece, jnp.float32),
            pltpu.VMEM((groups - 1,) + tile_part.shape, jnp.float32),
            dma((n,)),
            dma((n,)),
            dma((n - 1,)),
            dma((n - 1,)),
            dma((groups - 1,)),
            dma((groups - 1,)),
            dma((1,)),
            dma((1,)),
        ],
        compiler_params=pltpu.CompilerParams(
            collective_id=1, has_side_effects=True, vmem_limit_bytes=LIMIT
        ),
    )(mm_part, tile_part)


def pair_kernel(
    owned,
    pattern_ref,
    padding_ref,
    centers_ref,
    widths_ref,
    density_ref,
    prefactor_ref,
    atoms_ref,
    mm_ref,
    tile_ref,
    wide,
    near_atoms,
    acc,
    total,
):
    _, tiles, pairs = centers_ref.shape
    near = pattern_ref.shape[2]
    mm_ref[...] = jnp.zeros_like(mm_ref)
    slots = lax.broadcasted_iota(jnp.int32, (1, pairs), 1)
    part = lax.broadcasted_iota(jnp.int32, (32, 5 * 128), 0)
    column = lax.broadcasted_iota(jnp.int32, (32, 5 * 128), 1)
    spread = jnp.where(
        (part < 24) & ((part & 7) == (column >> 7)), 1.0, 0.0
    ).astype(jnp.bfloat16)
    for t in range(tiles):
        weight = jnp.where(
            slots < pairs - padding_ref[t],
            density_ref[t : t + 1, :] * prefactor_ref[t : t + 1, :],
            0.0,
        )
        rest = jnp.concatenate(
            [centers_ref[i, t : t + 1, :] for i in range(3)]
            + [widths_ref[t : t + 1, :], weight, jnp.zeros((3, pairs), jnp.float32)],
            axis=0,
        )
        pieces = []
        for _ in range(3):
            piece = rest.astype(jnp.bfloat16).astype(jnp.float32)
            pieces.append(piece)
            rest = rest - piece
        pieces.append(jnp.zeros_like(rest))
        pieces = jnp.concatenate(pieces, axis=0).astype(jnp.bfloat16)
        over = lax.dot_general(
            pieces, spread, (((0,), (0,)), ((), ())), preferred_element_type=jnp.float32
        )
        for i in range(5):
            wide[t, i] = over[:, 128 * i : 128 * (i + 1)]

    def one_tile(t, carry):
        valid = pairs - padding_ref[t]
        for n in range(near):
            b = pattern_ref[t, 0, n]
            shard = lax.div(b, owned)
            for i in range(3):
                row = b * 3 + shard * owned + i
                near_atoms[n, i] = jnp.broadcast_to(atoms_ref[pl.ds(row, 1), :], (8, 128))
            row = b + (shard + 1) * (3 * owned)
            near_atoms[n, 3] = jnp.broadcast_to(atoms_ref[pl.ds(row, 1), :], (8, 128))
            for i in range(3):
                acc[n, i] = jnp.zeros((8, 128), jnp.float32)
        steps = lax.div(valid + ROWS - 1, ROWS)

        def one_step(j, carry):
            row = pl.multiple_of(j * ROWS, ROWS)
            groups = [
                [wide[t, i, pl.ds(row + 8 * h, 8), :] for i in range(5)]
                for h in range(ROWS // 8)
            ]
            sums = [[None] * 3 for _ in groups]
            for n in range(near):
                x, y, z, q = (near_atoms[n, i] for i in range(4))
                here = [None] * 3
                for h, (cx, cy, cz, wid, wgt) in enumerate(groups):
                    dx, dy, dz = x - cx, y - cy, z - cz
                    s = (dx * dx + dy * dy) + (dz * dz + wid)
                    r = lax.rsqrt(s)
                    coef = (wgt * q) * (r * r * r)
                    for i, d in enumerate((dx, dy, dz)):
                        f = coef * d
                        here[i] = f if here[i] is None else here[i] + f
                        sums[h][i] = f if sums[h][i] is None else sums[h][i] + f
                for i in range(3):
                    acc[n, i] += here[i]
            for h in range(len(groups)):
                for i in range(3):
                    total[t, i, pl.ds(row + 8 * h, 8), :] = sums[h][i]
            return carry

        lax.fori_loop(0, steps, one_step, 0)
        for n in range(near):
            b = pattern_ref[t, 0, n]
            for i in range(3):
                mm_ref[pl.ds(b * 3 + i, 1), :] += jnp.sum(acc[n, i], axis=0, keepdims=True)
        return carry

    lax.fori_loop(0, tiles, one_tile, 0)
    ones = jnp.ones((16, 2 * 128), jnp.bfloat16)
    for t in range(tiles):
        for i in range(3):
            whole = total[t, i]
            high = whole.astype(jnp.bfloat16)
            low = (whole - high.astype(jnp.float32)).astype(jnp.bfloat16)
            line = lax.dot_general(
                ones,
                jnp.concatenate([high, low], axis=1),
                (((1,), (1,)), ((), ())),
                preferred_element_type=jnp.float32,
            )
            tile_ref[i, t : t + 1, :] = jnp.where(
                slots < pairs - padding_ref[t], -line[0:1, :], 0.0
            )


def interactions(owned, pattern, padding, centers, widths, density, prefactor, atoms):
    _, tiles, pairs = centers.shape
    near = pattern.shape[2]
    return pl.pallas_call(
        functools.partial(pair_kernel, owned),
        out_shape=(
            jax.ShapeDtypeStruct((atoms.shape[0] // 4 * 3, 128), jnp.float32),
            jax.ShapeDtypeStruct((3, tiles, pairs), jnp.float32),
        ),
        in_specs=[SMEM] * 2 + [VMEM] * 5,
        out_specs=(VMEM, VMEM),
        scratch_shapes=[
            pltpu.VMEM((tiles, 5, pairs, 128), jnp.float32),
            pltpu.VMEM((near, 4, 8, 128), jnp.float32),
            pltpu.VMEM((near, 3, 8, 128), jnp.float32),
            pltpu.VMEM((tiles, 3, pairs, 128), jnp.float32),
        ],
        compiler_params=pltpu.CompilerParams(vmem_limit_bytes=LIMIT),
    )(pattern, padding, centers, widths, density, prefactor, atoms)


def body(n, groups, centers, widths, density, prefactor, padding, pattern, mm_coords, mm_charges):
    owned, lanes = mm_coords.shape[0], mm_coords.shape[3]
    shard = jnp.concatenate(
        [mm_coords.reshape(3 * owned, lanes), mm_charges.reshape(owned, lanes)], axis=0
    )
    atoms = gather(n, shard)
    mm_part, tile_part = interactions(
        owned,
        pattern,
        padding,
        centers.transpose(1, 0, 2),
        widths,
        density,
        prefactor,
        atoms,
    )
    mm_part = mm_part.reshape(n, 2, 3 * owned // 2, lanes)
    mm_force, tile_force = reduce(n, groups, mm_part, tile_part)
    return (mm_force.reshape(mm_coords.shape), tile_force.transpose(1, 0, 2))


def solution(mesh):
    tiles = P(("groups", "pair", "sub"))
    placed = (
        tiles,
        tiles,
        tiles,
        tiles,
        tiles,
        P(("groups", "pair", "sub"), "mm", None),
        P(("groups", "pair"), "mm", None, None),
        P(("groups", "pair"), "mm", None),
    )
    return jax.shard_map(
        functools.partial(body, mesh.shape["pair"], mesh.shape["mm"]),
        mesh=mesh,
        in_specs=placed,
        out_specs=(P(("groups", "pair"), "mm", None, None), tiles),
        check_vma=False,
    )
```

```python
import functools

import jax
import jax.numpy as jnp
from jax import lax
from jax.experimental import pallas as pl
from jax.experimental.pallas import tpu as pltpu
from jax.sharding import PartitionSpec as P

ROWS = 16
LIMIT = 24 * 1024 * 1024
VMEM = pl.BlockSpec(memory_space=pltpu.VMEM)
SMEM = pl.BlockSpec(memory_space=pltpu.SMEM)


def remote(src, dst, send, recv, **where):
    return pltpu.make_async_remote_copy(
        src_ref=src,
        dst_ref=dst,
        send_sem=send,
        recv_sem=recv,
        device_id=where,
        device_id_type=pl.DeviceIdType.MESH,
    )


def greet(peers):
    barrier = pltpu.get_barrier_semaphore()
    for where in peers:
        pl.semaphore_signal(
            barrier, inc=1, device_id=where, device_id_type=pl.DeviceIdType.MESH
        )
    pl.semaphore_wait(barrier, len(peers))


def gather_kernel(n, shard_ref, out_ref, send, recv, core_send, core_recv):
    owned = shard_ref.shape[0]
    half = owned // 2
    p, s = lax.axis_index("pair"), lax.axis_index("sub")
    peers = [lax.rem(p + k, n) for k in range(1, n)]
    greet([{"pair": q} for q in peers] + [{"sub": 1 - s}])

    def part(q):
        return out_ref.at[pl.ds(pl.multiple_of(q * owned + s * half, half), half)]

    out = [
        remote(
            shard_ref.at[pl.ds(pl.multiple_of(s * half, half), half)],
            part(p),
            send.at[k],
            recv.at[k],
            pair=q,
        )
        for k, q in enumerate(peers)
    ]
    for copy in out:
        copy.start()
    out_ref[pl.ds(pl.multiple_of(p * owned, owned), owned)] = shard_ref[...]
    across = []
    for k in range(n - 1):
        out[k].wait_recv()
        q = lax.rem(p + n - 1 - k, n)
        copy = remote(part(q), part(q), core_send.at[k], core_recv.at[k], sub=1 - s)
        copy.start()
        across.append(copy)
    for copy in across:
        copy.wait()
    for copy in out:
        copy.wait_send()


def gather(n, shard):
    return pl.pallas_call(
        functools.partial(gather_kernel, n),
        out_shape=jax.ShapeDtypeStruct((n * shard.shape[0],) + shard.shape[1:], jnp.float32),
        in_specs=[VMEM],
        out_specs=VMEM,
        scratch_shapes=[pltpu.SemaphoreType.DMA((n - 1,))] * 4,
        compiler_params=pltpu.CompilerParams(
            collective_id=0, has_side_effects=True, vmem_limit_bytes=LIMIT
        ),
    )(shard)


def reduce_kernel(
    n,
    groups,
    part_ref,
    tile_ref,
    mm_ref,
    sum_ref,
    swapped,
    summed,
    landed,
    tile_landed,
    core_send,
    core_recv,
    send,
    recv,
    tile_send,
    tile_recv,
    last_send,
    last_recv,
):
    p, m, s = (lax.axis_index(a) for a in ("pair", "mm", "sub"))
    peers = [lax.rem(p + k, n) for k in range(1, n)] + [p]
    others = [lax.rem(m + k, groups) for k in range(1, groups)]
    greet([{"pair": q} for q in peers[:-1]] + [{"sub": 1 - s}] + [{"mm": g} for g in others])
    across = [
        remote(part_ref.at[q, 1 - s], swapped.at[k], core_send.at[k], core_recv.at[k], sub=1 - s)
        for k, q in enumerate(peers)
    ]
    for copy in across:
        copy.start()
    tiles = [
        remote(tile_ref, tile_landed.at[k], tile_send.at[k], tile_recv.at[k], mm=g)
        for k, g in enumerate(others)
    ]
    for copy in tiles:
        copy.start()
    out = []
    for k, q in enumerate(peers):
        across[k].wait_recv()
        if k < n - 1:
            summed[k] = part_ref[q, s] + swapped[k]
            copy = remote(summed.at[k], landed.at[k], send.at[k], recv.at[k], pair=q)
            copy.start()
            out.append(copy)
        else:
            total = part_ref[q, s] + swapped[k]
    for k, copy in enumerate(out):
        copy.wait_recv()
        total = total + landed[k]
    mm_ref[s] = total
    last = remote(mm_ref.at[s], mm_ref.at[s], last_send.at[0], last_recv.at[0], sub=1 - s)
    last.start()
    tile_total = tile_ref[...]
    for k, copy in enumerate(tiles):
        copy.wait_recv()
        tile_total = tile_total + tile_landed[k]
    sum_ref[...] = tile_total
    last.wait()
    for copy in across + out + tiles:
        copy.wait_send()


def reduce(n, groups, mm_part, tile_part):
    piece = mm_part.shape[2:]
    dma = pltpu.SemaphoreType.DMA
    return pl.pallas_call(
        functools.partial(reduce_kernel, n, groups),
        out_shape=(
            jax.ShapeDtypeStruct((2,) + piece, jnp.float32),
            jax.ShapeDtypeStruct(tile_part.shape, jnp.float32),
        ),
        in_specs=[VMEM] * 2,
        out_specs=(VMEM, VMEM),
        scratch_shapes=[
            pltpu.VMEM((n,) + piece, jnp.float32),
            pltpu.VMEM((n - 1,) + piece, jnp.float32),
            pltpu.VMEM((n - 1,) + piece, jnp.float32),
            pltpu.VMEM((groups - 1,) + tile_part.shape, jnp.float32),
            dma((n,)),
            dma((n,)),
            dma((n - 1,)),
            dma((n - 1,)),
            dma((groups - 1,)),
            dma((groups - 1,)),
            dma((1,)),
            dma((1,)),
        ],
        compiler_params=pltpu.CompilerParams(
            collective_id=1, has_side_effects=True, vmem_limit_bytes=LIMIT
        ),
    )(mm_part, tile_part)


def pair_kernel(
    pattern_ref,
    padding_ref,
    centers_ref,
    widths_ref,
    density_ref,
    prefactor_ref,
    atoms_ref,
    mm_ref,
    tile_ref,
    wide,
    near_atoms,
    acc,
    total,
):
    _, tiles, pairs = centers_ref.shape
    near = pattern_ref.shape[2]
    half = mm_ref.shape[1]
    mm_ref[...] = jnp.zeros_like(mm_ref)
    slots = lax.broadcasted_iota(jnp.int32, (1, pairs), 1)
    part = lax.broadcasted_iota(jnp.int32, (32, 5 * 128), 0)
    column = lax.broadcasted_iota(jnp.int32, (32, 5 * 128), 1)
    spread = jnp.where(
        (part < 24) & ((part & 7) == (column >> 7)), 1.0, 0.0
    ).astype(jnp.bfloat16)
    for t in range(tiles):
        weight = jnp.where(
            slots < pairs - padding_ref[t],
            density_ref[t : t + 1, :] * prefactor_ref[t : t + 1, :],
            0.0,
        )
        rest = jnp.concatenate(
            [centers_ref[i, t : t + 1, :] for i in range(3)]
            + [widths_ref[t : t + 1, :], weight, jnp.zeros((3, pairs), jnp.float32)],
            axis=0,
        )
        pieces = []
        for _ in range(3):
            piece = rest.astype(jnp.bfloat16).astype(jnp.float32)
            pieces.append(piece)
            rest = rest - piece
        pieces.append(jnp.zeros_like(rest))
        pieces = jnp.concatenate(pieces, axis=0).astype(jnp.bfloat16)
        over = lax.dot_general(
            pieces, spread, (((0,), (0,)), ((), ())), preferred_element_type=jnp.float32
        )
        for i in range(5):
            wide[t, i] = over[:, 128 * i : 128 * (i + 1)]

    def one_tile(t, carry):
        valid = pairs - padding_ref[t]
        for n in range(near):
            b = pattern_ref[t, 0, n]
            for i in range(4):
                near_atoms[n, i] = jnp.broadcast_to(atoms_ref[b, i : i + 1, :], (8, 128))
            for i in range(3):
                acc[n, i] = jnp.zeros((8, 128), jnp.float32)
        steps = lax.div(valid + ROWS - 1, ROWS)

        def one_step(j, carry):
            row = pl.multiple_of(j * ROWS, ROWS)
            groups = [
                [wide[t, i, pl.ds(row + 8 * h, 8), :] for i in range(5)]
                for h in range(ROWS // 8)
            ]
            sums = [[None] * 3 for _ in groups]
            for n in range(near):
                x, y, z, q = (near_atoms[n, i] for i in range(4))
                here = [None] * 3
                for h, (cx, cy, cz, wid, wgt) in enumerate(groups):
                    dx, dy, dz = x - cx, y - cy, z - cz
                    s = (dx * dx + dy * dy) + (dz * dz + wid)
                    r = lax.rsqrt(s)
                    coef = (wgt * q) * (r * r * r)
                    for i, d in enumerate((dx, dy, dz)):
                        f = coef * d
                        here[i] = f if here[i] is None else here[i] + f
                        sums[h][i] = f if sums[h][i] is None else sums[h][i] + f
                for i in range(3):
                    acc[n, i] += here[i]
            for h in range(len(groups)):
                for i in range(3):
                    total[t, i, pl.ds(row + 8 * h, 8), :] = sums[h][i]
            return carry

        lax.fori_loop(0, steps, one_step, 0)
        for n in range(near):
            b = pattern_ref[t, 0, n]
            piece = lax.div(b, half)
            row = b - piece * half
            for i in range(3):
                mm_ref[piece * 3 + i, pl.ds(row, 1), :] += jnp.sum(
                    acc[n, i], axis=0, keepdims=True
                )
        return carry

    lax.fori_loop(0, tiles, one_tile, 0)
    ones = jnp.ones((16, 2 * 128), jnp.bfloat16)
    for t in range(tiles):
        for i in range(3):
            whole = total[t, i]
            high = whole.astype(jnp.bfloat16)
            low = (whole - high.astype(jnp.float32)).astype(jnp.bfloat16)
            line = lax.dot_general(
                ones,
                jnp.concatenate([high, low], axis=1),
                (((1,), (1,)), ((), ())),
                preferred_element_type=jnp.float32,
            )
            tile_ref[i, t : t + 1, :] = jnp.where(
                slots < pairs - padding_ref[t], -line[0:1, :], 0.0
            )


def interactions(half, pattern, padding, centers, widths, density, prefactor, atoms):
    _, tiles, pairs = centers.shape
    near = pattern.shape[2]
    return pl.pallas_call(
        pair_kernel,
        out_shape=(
            jax.ShapeDtypeStruct((atoms.shape[0] // half * 3, half, 128), jnp.float32),
            jax.ShapeDtypeStruct((3, tiles, pairs), jnp.float32),
        ),
        in_specs=[SMEM] * 2 + [VMEM] * 5,
        out_specs=(VMEM, VMEM),
        scratch_shapes=[
            pltpu.VMEM((tiles, 5, pairs, 128), jnp.float32),
            pltpu.VMEM((near, 4, 8, 128), jnp.float32),
            pltpu.VMEM((near, 3, 8, 128), jnp.float32),
            pltpu.VMEM((tiles, 3, pairs, 128), jnp.float32),
        ],
        compiler_params=pltpu.CompilerParams(vmem_limit_bytes=LIMIT),
    )(pattern, padding, centers, widths, density, prefactor, atoms)


def body(n, groups, centers, widths, density, prefactor, padding, pattern, mm_coords, mm_charges):
    owned = mm_coords.shape[0]
    half = owned // 2
    atoms = gather(n, jnp.concatenate([mm_coords[:, 0], mm_charges], axis=1))
    mm_part, tile_part = interactions(
        half, pattern, padding, centers.transpose(1, 0, 2), widths, density, prefactor, atoms
    )
    mm_part = mm_part.reshape(n, 2, 3, half, mm_coords.shape[3])
    mm_force, tile_force = reduce(n, groups, mm_part, tile_part)
    mm_force = mm_force.transpose(0, 2, 1, 3).reshape(mm_coords.shape)
    return (mm_force, tile_force.transpose(1, 0, 2))


def solution(mesh):
    tiles = P(("groups", "pair", "sub"))
    placed = (
        tiles,
        tiles,
        tiles,
        tiles,
        tiles,
        P(("groups", "pair", "sub"), "mm", None),
        P(("groups", "pair"), "mm", None, None),
        P(("groups", "pair"), "mm", None),
    )
    return jax.shard_map(
        functools.partial(body, mesh.shape["pair"], mesh.shape["mm"]),
        mesh=mesh,
        in_specs=placed,
        out_specs=(P(("groups", "pair"), "mm", None, None), tiles),
        check_vma=False,
    )
```

```python
import functools

import jax
import jax.numpy as jnp
from jax import lax
from jax.experimental import pallas as pl
from jax.experimental.pallas import tpu as pltpu
from jax.sharding import PartitionSpec as P

ROWS = 16
LIMIT = 48 * 1024 * 1024
VMEM = pl.BlockSpec(memory_space=pltpu.VMEM)
SMEM = pl.BlockSpec(memory_space=pltpu.SMEM)


def remote(src, dst, send, recv, **where):
    return pltpu.make_async_remote_copy(
        src_ref=src,
        dst_ref=dst,
        send_sem=send,
        recv_sem=recv,
        device_id=where,
        device_id_type=pl.DeviceIdType.MESH,
    )


def greet(peers):
    barrier = pltpu.get_barrier_semaphore()
    for where in peers:
        pl.semaphore_signal(
            barrier, inc=1, device_id=where, device_id_type=pl.DeviceIdType.MESH
        )
    pl.semaphore_wait(barrier, len(peers))


def gather_kernel(n, coords_ref, charges_ref, out_ref, send, recv, core_send, core_recv):
    owned = coords_ref.shape[0]
    half = owned // 2
    p, s = lax.axis_index("pair"), lax.axis_index("sub")
    mine = pl.multiple_of(p * owned, owned)
    out_ref[pl.ds(mine, owned), 0:3, :] = coords_ref[:, 0]
    out_ref[pl.ds(mine, owned), 3:4, :] = charges_ref[...]
    offsets = sorted(range(1, n), key=lambda k: -min(k, n - k))
    peers = [lax.rem(p + k, n) for k in offsets]
    greet([{"pair": q} for q in peers] + [{"sub": 1 - s}])

    def part(q):
        return out_ref.at[pl.ds(pl.multiple_of(q * owned + s * half, half), half)]

    out = [
        remote(part(p), part(p), send.at[k], recv.at[k], pair=q) for k, q in enumerate(peers)
    ]
    for copy in out:
        copy.start()
    across = []
    for k in range(n - 1):
        out[k].wait_recv()
        q = lax.rem(p + n - offsets[k], n)
        copy = remote(part(q), part(q), core_send.at[k], core_recv.at[k], sub=1 - s)
        copy.start()
        across.append(copy)
    for copy in across:
        copy.wait()
    for copy in out:
        copy.wait_send()


def gather(n, coords, charges):
    owned, _, _, atoms = coords.shape
    return pl.pallas_call(
        functools.partial(gather_kernel, n),
        out_shape=jax.ShapeDtypeStruct((n * owned, 4, atoms), jnp.float32),
        in_specs=[VMEM] * 2,
        out_specs=VMEM,
        scratch_shapes=[pltpu.SemaphoreType.DMA((n - 1,))] * 4,
        compiler_params=pltpu.CompilerParams(
            collective_id=0, has_side_effects=True, vmem_limit_bytes=LIMIT
        ),
    )(coords, charges)


def reduce_kernel(
    n,
    groups,
    part_ref,
    tile_ref,
    mm_ref,
    sum_ref,
    swapped,
    summed,
    landed,
    tile_landed,
    core_send,
    core_recv,
    send,
    recv,
    tile_send,
    tile_recv,
    last_send,
    last_recv,
):
    p, m, s = (lax.axis_index(a) for a in ("pair", "mm", "sub"))
    offsets = sorted(range(1, n), key=lambda k: -min(k, n - k))
    peers = [lax.rem(p + k, n) for k in offsets] + [p]
    others = [lax.rem(m + k, groups) for k in range(1, groups)]
    greet([{"pair": q} for q in peers[:-1]] + [{"sub": 1 - s}] + [{"mm": g} for g in others])
    across = [
        remote(part_ref.at[q, 1 - s], swapped.at[k], core_send.at[k], core_recv.at[k], sub=1 - s)
        for k, q in enumerate(peers)
    ]
    for copy in across:
        copy.start()
    tiles = [
        remote(tile_ref, tile_landed.at[k], tile_send.at[k], tile_recv.at[k], mm=g)
        for k, g in enumerate(others)
    ]
    for copy in tiles:
        copy.start()
    out = []
    for k, q in enumerate(peers):
        across[k].wait_recv()
        if k < n - 1:
            summed[k] = part_ref[q, s] + swapped[k]
            copy = remote(summed.at[k], landed.at[k], send.at[k], recv.at[k], pair=q)
            copy.start()
            out.append(copy)
        else:
            total = part_ref[q, s] + swapped[k]
    for k, copy in enumerate(out):
        copy.wait_recv()
        total = total + landed[k]
    mm_ref[s] = total
    last = remote(mm_ref.at[s], mm_ref.at[s], last_send.at[0], last_recv.at[0], sub=1 - s)
    last.start()
    tile_total = tile_ref[...]
    for k, copy in enumerate(tiles):
        copy.wait_recv()
        tile_total = tile_total + tile_landed[k]
    sum_ref[...] = tile_total
    last.wait()
    for copy in across + out + tiles:
        copy.wait_send()


def reduce(n, groups, mm_part, tile_part):
    piece = mm_part.shape[2:]
    dma = pltpu.SemaphoreType.DMA
    return pl.pallas_call(
        functools.partial(reduce_kernel, n, groups),
        out_shape=(
            jax.ShapeDtypeStruct((2,) + piece, jnp.float32),
            jax.ShapeDtypeStruct(tile_part.shape, jnp.float32),
        ),
        in_specs=[VMEM] * 2,
        out_specs=(VMEM, VMEM),
        scratch_shapes=[
            pltpu.VMEM((n,) + piece, jnp.float32),
            pltpu.VMEM((n - 1,) + piece, jnp.float32),
            pltpu.VMEM((n - 1,) + piece, jnp.float32),
            pltpu.VMEM((groups - 1,) + tile_part.shape, jnp.float32),
            dma((n,)),
            dma((n,)),
            dma((n - 1,)),
            dma((n - 1,)),
            dma((groups - 1,)),
            dma((groups - 1,)),
            dma((1,)),
            dma((1,)),
        ],
        compiler_params=pltpu.CompilerParams(
            collective_id=1, has_side_effects=True, vmem_limit_bytes=LIMIT
        ),
    )(mm_part, tile_part)


def pair_kernel(
    pattern_ref,
    padding_ref,
    centers_ref,
    widths_ref,
    density_ref,
    prefactor_ref,
    atoms_ref,
    mm_ref,
    tile_ref,
    wide,
    near_atoms,
    acc,
    total,
):
    tiles, _, pairs = centers_ref.shape
    near = pattern_ref.shape[2]
    half = mm_ref.shape[1]
    mm_ref[...] = jnp.zeros_like(mm_ref)
    slots = lax.broadcasted_iota(jnp.int32, (1, pairs), 1)
    part = lax.broadcasted_iota(jnp.int32, (32, 5 * 128), 0)
    column = lax.broadcasted_iota(jnp.int32, (32, 5 * 128), 1)
    spread = jnp.where(
        (part < 24) & ((part & 7) == (column >> 7)), 1.0, 0.0
    ).astype(jnp.bfloat16)
    for t in range(tiles):
        weight = jnp.where(
            slots < pairs - padding_ref[t],
            density_ref[t : t + 1, :] * prefactor_ref[t : t + 1, :],
            0.0,
        )
        rest = jnp.concatenate(
            [centers_ref[t], widths_ref[t : t + 1, :], weight, jnp.zeros((3, pairs), jnp.float32)],
            axis=0,
        )
        pieces = []
        for _ in range(3):
            piece = rest.astype(jnp.bfloat16).astype(jnp.float32)
            pieces.append(piece)
            rest = rest - piece
        pieces.append(jnp.zeros_like(rest))
        pieces = jnp.concatenate(pieces, axis=0).astype(jnp.bfloat16)
        over = lax.dot_general(
            pieces, spread, (((0,), (0,)), ((), ())), preferred_element_type=jnp.float32
        )
        for i in range(5):
            wide[t, i] = over[:, 128 * i : 128 * (i + 1)]

    def one_tile(t, carry):
        valid = pairs - padding_ref[t]
        for n in range(near):
            b = pattern_ref[t, 0, n]
            for i in range(4):
                near_atoms[n, i] = jnp.broadcast_to(atoms_ref[b, i : i + 1, :], (8, 128))
            for i in range(3):
                acc[n, i] = jnp.zeros((8, 128), jnp.float32)
        steps = lax.div(valid + ROWS - 1, ROWS)

        def one_step(j, carry):
            row = pl.multiple_of(j * ROWS, ROWS)
            groups = [
                [wide[t, i, pl.ds(row + 8 * h, 8), :] for i in range(5)]
                for h in range(ROWS // 8)
            ]
            sums = [[None] * 3 for _ in groups]
            for n in range(near):
                x, y, z, q = (near_atoms[n, i] for i in range(4))
                here = [None] * 3
                for h, (cx, cy, cz, wid, wgt) in enumerate(groups):
                    dx, dy, dz = x - cx, y - cy, z - cz
                    s = (dx * dx + dy * dy) + (dz * dz + wid)
                    r = lax.rsqrt(s)
                    coef = (wgt * q) * (r * r * r)
                    for i, d in enumerate((dx, dy, dz)):
                        f = coef * d
                        here[i] = f if here[i] is None else here[i] + f
                        sums[h][i] = f if sums[h][i] is None else sums[h][i] + f
                for i in range(3):
                    acc[n, i] += here[i]
            for h in range(len(groups)):
                for i in range(3):
                    total[t, i, pl.ds(row + 8 * h, 8), :] = sums[h][i]
            return carry

        lax.fori_loop(0, steps, one_step, 0)
        for n in range(near):
            b = pattern_ref[t, 0, n]
            piece = lax.div(b, half)
            row = b - piece * half
            for i in range(3):
                mm_ref[piece * 3 + i, pl.ds(row, 1), :] += jnp.sum(
                    acc[n, i], axis=0, keepdims=True
                )
        return carry

    lax.fori_loop(0, tiles, one_tile, 0)
    ones = jnp.ones((16, 2 * 128), jnp.bfloat16)
    for t in range(tiles):
        for i in range(3):
            whole = total[t, i]
            high = whole.astype(jnp.bfloat16)
            low = (whole - high.astype(jnp.float32)).astype(jnp.bfloat16)
            line = lax.dot_general(
                ones,
                jnp.concatenate([high, low], axis=1),
                (((1,), (1,)), ((), ())),
                preferred_element_type=jnp.float32,
            )
            tile_ref[i, t : t + 1, :] = jnp.where(
                slots < pairs - padding_ref[t], -line[0:1, :], 0.0
            )


def interactions(half, pattern, padding, centers, widths, density, prefactor, atoms):
    tiles, _, pairs = centers.shape
    near = pattern.shape[2]
    return pl.pallas_call(
        pair_kernel,
        out_shape=(
            jax.ShapeDtypeStruct((atoms.shape[0] // half * 3, half, 128), jnp.float32),
            jax.ShapeDtypeStruct((3, tiles, pairs), jnp.float32),
        ),
        in_specs=[SMEM] * 2 + [VMEM] * 5,
        out_specs=(VMEM, VMEM),
        scratch_shapes=[
            pltpu.VMEM((tiles, 5, pairs, 128), jnp.float32),
            pltpu.VMEM((near, 4, 8, 128), jnp.float32),
            pltpu.VMEM((near, 3, 8, 128), jnp.float32),
            pltpu.VMEM((tiles, 3, pairs, 128), jnp.float32),
        ],
        compiler_params=pltpu.CompilerParams(vmem_limit_bytes=LIMIT),
    )(pattern, padding, centers, widths, density, prefactor, atoms)


def body(n, groups, centers, widths, density, prefactor, padding, pattern, mm_coords, mm_charges):
    owned = mm_coords.shape[0]
    half = owned // 2
    atoms = gather(n, mm_coords, mm_charges)
    mm_part, tile_part = interactions(
        half, pattern, padding, centers, widths, density, prefactor, atoms
    )
    mm_part = mm_part.reshape(n, 2, 3, half, mm_coords.shape[3])
    mm_force, tile_force = reduce(n, groups, mm_part, tile_part)
    mm_force = mm_force.transpose(0, 2, 1, 3).reshape(mm_coords.shape)
    return (mm_force, tile_force.transpose(1, 0, 2))


def solution(mesh):
    tiles = P(("groups", "pair", "sub"))
    placed = (
        tiles,
        tiles,
        tiles,
        tiles,
        tiles,
        P(("groups", "pair", "sub"), "mm", None),
        P(("groups", "pair"), "mm", None, None),
        P(("groups", "pair"), "mm", None),
    )
    return jax.shard_map(
        functools.partial(body, mesh.shape["pair"], mesh.shape["mm"]),
        mesh=mesh,
        in_specs=placed,
        out_specs=(P(("groups", "pair"), "mm", None, None), tiles),
        check_vma=False,
    )
```
